32 devices in a mesh: groups: 2 (over y), tile: 4 (over z), rep: 2 (over x), sub: 2 (over core).
Axes of the slice: x: 2, y: 2, z: 4, core: 2. Of those that a mesh axis runs over, the one named last changes fastest.
Arguments:
- amplitudes: bfloat16 [4096, 2048], P(('groups', 'tile', 'sub'), 'rep'), parts along dimension 0, may hold values from -6 to 6
- amp_mask: int32 [32, 16], P(('groups', 'tile', 'sub'), 'rep'), parts along dimension 0, may hold values 0 or 1
- integrals: bfloat16 [2048, 4096], P('rep', 'tile'), may hold values from -0.125 to 0.125
- int_mask: int32 [16, 32], P('rep', 'tile'), may hold values 0 or 1
- owner_map: int32 [8], P('groups'), parts along dimension 0, may hold values from 0 to 3
Outputs:
- ladder: bfloat16 [8, 512, 4096], P('groups', 'sub', ('tile', 'rep')), parts along dimension 0
The draws below stay inside these ranges and needn't reach their ends.
There are 2 independent parts, one for each index of `groups`. The reference program is written for one: setup_inputs(seed, part) draws one part's arguments, and reference() takes and returns one part's arrays. A program takes and returns all parts, laid end to end along the dimension named above; an argument that names none is the same for every part. Nothing has to cross between parts.
Inputs may be any that keep to these rules, and one draw needn't show every extreme that they name: `owner_map`: block owners, any of them, repeats allowed.
All inputs are finite; a program needn't handle non-finite values. No bound on the sum of `amp_mask` or of `int_mask` on one device may be relied on, other than what follows from the above.
Results may differ from the reference program's by a relative error of at most 0.0052.
Values may be sent and summed in bfloat16 or wider, within the bound.
A program may use at most 64 MiB of HBM per device.

```python
import jax
import jax.numpy as jnp
from jax import lax

TILE = 128
CD_DEV = 1024
STEPS = 4
PAIRS = 512
NPAIR = 2048
NCD = 2048
NAB = 4096
N_TILE = 4
N_REP = 2


def plant(entries, stream_key, smallest, top_value):
    shape = entries.shape
    spot = [jax.random.randint(jax.random.fold_in(stream_key, axis), (), 0, shape[axis]) for axis in range(len(shape))]
    entries = entries.at[tuple(spot)].set(smallest)
    longest = shape.index(max(shape))
    spot[longest] = (spot[longest] + 1) % shape[longest]
    return entries.at[tuple(spot)].set(top_value)


def steps_of(own_key, extent, split, least, top_value):
    loudness = 1.0
    for axis_at, shards_of in split:
        heights = jax.random.uniform(jax.random.fold_in(jax.random.fold_in(own_key, 6), axis_at), (shards_of,), jnp.float32, least / len(split), top_value / len(split))
        loudness = loudness * jnp.repeat(jnp.exp(heights), extent[axis_at] // shards_of).reshape((-1,) + (1,) * (len(extent) - 1 - axis_at))
    return loudness


def centred(key, dims, spread, most, shards=(), held_as=jnp.bfloat16):
    array = jax.random.normal(key, dims, jnp.float32) * spread
    if len(shards) > 0:
        array = steps_of(key, dims, shards, -0.22, 0.18) * array
    return jnp.clip(array, min=-most, max=most).astype(held_as)


def setup_inputs(seed: int = 0, part: int = 0) -> dict:
    streams_of = jax.random.split(jax.random.key(seed), 6)
    own_keys = jax.random.split(jax.random.fold_in(streams_of[5], part), 6)
    return {
        "amplitudes": centred(own_keys[0], (NPAIR, NCD), 1.0, 6.0, ((0, 8), (1, 2))),
        "amp_mask": plant((jax.random.randint(own_keys[1], (NPAIR // TILE, NCD // TILE), 0, 3) < 2).astype(jnp.int32), jax.random.fold_in(own_keys[1], 1), 0, 1),
        "integrals": centred(streams_of[2], (NCD, NAB), NCD ** -0.5, 0.125, ((0, 2), (1, 4))),
        "int_mask": plant((jax.random.randint(streams_of[3], (NCD // TILE, NAB // TILE), 0, 3) < 2).astype(jnp.int32), jax.random.fold_in(streams_of[3], 1), 0, 1),
        "owner_map": plant(jax.random.randint(own_keys[4], (STEPS,), 0, N_TILE), jax.random.fold_in(own_keys[4], 1), 0, N_TILE - 1).astype(jnp.int32),
    }


def expand_mask(mask):
    big = jnp.repeat(jnp.repeat(mask, TILE, axis=0), TILE, axis=1)
    return big.astype(jnp.bfloat16)


def reference(amplitudes, amp_mask, integrals, int_mask, owner_map):
    masked_amp = amplitudes * expand_mask(amp_mask)
    masked_int = integrals * expand_mask(int_mask)
    results = []
    for step in range(STEPS):
        start = (owner_map[step] * PAIRS).astype(jnp.int32)
        rows = lax.dynamic_slice_in_dim(masked_amp, start, PAIRS, 0)
        total = jnp.zeros((PAIRS, NAB), jnp.float32)
        for part_index in range(N_REP):
            lower = part_index * CD_DEV
            piece = jnp.dot(rows[:, lower:lower + CD_DEV], masked_int[lower:lower + CD_DEV, :], preferred_element_type=jnp.float32)
            total = total + piece.astype(jnp.bfloat16).astype(jnp.float32)
        results.append(total.astype(jnp.bfloat16))
    return jnp.stack(results, axis=0)
```

```python
import functools

import jax
import jax.numpy as jnp
from jax import lax
from jax.experimental import pallas as pl
from jax.experimental.pallas import tpu as pltpu
from jax.sharding import PartitionSpec as P

TILE = 128
CHUNKS = 4
MESH = pl.DeviceIdType.MESH


def expand_mask(mask):
    big = jnp.repeat(jnp.repeat(mask, TILE, axis=0), TILE, axis=1)
    return big.astype(jnp.bfloat16)


def from_root(block, axis, source):
    block = jnp.where(lax.axis_index(axis) == source, block, jnp.zeros_like(block))
    return lax.psum(block, axis)


def stepwise(amplitudes, amp_mask, integrals, int_mask, owner_map):
    masked_amp = amplitudes * expand_mask(amp_mask)
    masked_int = integrals * expand_mask(int_mask)
    results = []
    for step in range(owner_map.shape[0]):
        block_rows = from_root(masked_amp, "tile", owner_map[step])
        partial_value = jnp.dot(block_rows, masked_int, preferred_element_type=jnp.float32)
        summed = lax.psum_scatter(
            partial_value.astype(jnp.bfloat16), "rep", scatter_dimension=1, tiled=True
        )
        results.append(summed)
    return jnp.stack(results, axis=0)


def tile_scale(mask_ref, i, j, shape):
    return jnp.full(shape, mask_ref[i, j].astype(jnp.float32), jnp.float32).astype(jnp.bfloat16)


def gather_kernel(
    n, reps, amp_mask, int_mask, amp_hbm, int_hbm, out_ref,
    blocks, ints, mine, sent, got,
    load_sem, up_send, up_recv, down_send, down_recv, x_send, x_recv,
):
    z = lax.axis_index("tile")
    x = lax.axis_index("rep")
    rows, depth = amp_hbm.shape
    part = rows // CHUNKS
    width = int_hbm.shape[1] // reps

    load_amp = pltpu.make_async_copy(amp_hbm, blocks.at[z], load_sem.at[0])
    load_int = pltpu.make_async_copy(int_hbm, ints, load_sem.at[1])
    load_amp.start()
    load_int.start()

    barrier = pltpu.get_barrier_semaphore()

    @pl.when(z > 0)
    def _():
        pl.semaphore_signal(barrier, inc=1, device_id={"tile": z - 1}, device_id_type=MESH)

    @pl.when(z < n - 1)
    def _():
        pl.semaphore_signal(barrier, inc=1, device_id={"tile": z + 1}, device_id_type=MESH)

    for k in range(1, reps):
        pl.semaphore_signal(barrier, inc=1, device_id={"rep": lax.rem(x + k, reps)}, device_id_type=MESH)
    pl.semaphore_wait(barrier, jnp.where(z > 0, 1, 0) + jnp.where(z < n - 1, 1, 0) + (reps - 1))

    def span(c):
        return pl.ds(pl.multiple_of(c * part, part), part)

    def up(b, c):
        piece = blocks.at[b, span(c)]
        return pltpu.make_async_remote_copy(
            src_ref=piece, dst_ref=piece, send_sem=up_send.at[b, c], recv_sem=up_recv.at[b, c],
            device_id={"tile": z + 1}, device_id_type=MESH)

    def down(b, c):
        piece = blocks.at[b, span(c)]
        return pltpu.make_async_remote_copy(
            src_ref=piece, dst_ref=piece, send_sem=down_send.at[b, c], recv_sem=down_recv.at[b, c],
            device_id={"tile": z - 1}, device_id_type=MESH)

    def across(k, b, c):
        return pltpu.make_async_remote_copy(
            src_ref=sent.at[k - 1, b, span(c)], dst_ref=got.at[k - 1, b, span(c)],
            send_sem=x_send.at[k - 1, b, c], recv_sem=x_recv.at[k - 1, b, c],
            device_id={"rep": lax.rem(x + k, reps)}, device_id_type=MESH)

    def columns(r):
        return pl.ds(pl.multiple_of(r * width, width), width)

    def compute(b, c):
        for k in range(1, reps):
            sent[k - 1, b, span(c), :] = jnp.dot(
                blocks[b, span(c), :], ints[:, columns(lax.rem(x + k, reps))],
                preferred_element_type=jnp.float32).astype(jnp.bfloat16)
            across(k, b, c).start()
        mine[b, span(c), :] = jnp.dot(
            blocks[b, span(c), :], ints[:, columns(x)],
            preferred_element_type=jnp.float32).astype(jnp.bfloat16)

    def finish(b, c):
        total = mine[b, span(c), :].astype(jnp.float32)
        for k in range(1, reps):
            across(k, b, c).wait_recv()
            total = total + got[k - 1, b, span(c), :].astype(jnp.float32)
        out_ref[b, span(c), :] = total.astype(jnp.bfloat16)

    load_amp.wait()
    for c in range(CHUNKS):
        at = slice(c * part, (c + 1) * part)
        for j in range(depth // TILE):
            here = slice(j * TILE, (j + 1) * TILE)
            scale = tile_scale(amp_mask, c * part // TILE, j, (part, TILE))
            blocks[z, at, here] = blocks[z, at, here] * scale

        @pl.when(z < n - 1)
        def _():
            up(z, c).start()

        @pl.when(z > 0)
        def _():
            down(z, c).start()

    load_int.wait()
    for j in range(int_hbm.shape[1] // TILE):
        here = slice(j * TILE, (j + 1) * TILE)

        @pl.loop(0, depth // TILE)
        def _(i):
            at = pl.ds(pl.multiple_of(i * TILE, TILE), TILE)
            ints[at, here] = ints[at, here] * tile_scale(int_mask, i, j, (TILE, TILE))

    @pl.loop(0, CHUNKS)
    def _(c):
        compute(z, c)

    @pl.loop(1, n)
    def _(d):
        lower, upper = z - d, z + d

        @pl.loop(0, CHUNKS)
        def _(c):
            @pl.when(lower >= 0)
            def _():
                up(lower, c).wait_recv()

                @pl.when(z < n - 1)
                def _():
                    up(lower, c).start()

            @pl.when(upper < n)
            def _():
                down(upper, c).wait_recv()

                @pl.when(z > 0)
                def _():
                    down(upper, c).start()

            @pl.when(lower >= 0)
            def _():
                compute(lower, c)

            @pl.when(upper < n)
            def _():
                compute(upper, c)

            @pl.when(lower + 1 >= 0)
            def _():
                finish(lower + 1, c)

            @pl.when((upper - 1 < n) & (d > 1))
            def _():
                finish(upper - 1, c)

    @pl.loop(0, CHUNKS)
    def _(c):
        @pl.when(z == n - 1)
        def _():
            finish(0, c)

        @pl.when(z == 0)
        def _():
            finish(n - 1, c)

    @pl.loop(0, n)
    def _(b):
        @pl.loop(0, CHUNKS)
        def _(c):
            for k in range(1, reps):
                across(k, b, c).wait_send()

            @pl.when((b <= z) & (z < n - 1))
            def _():
                up(b, c).wait_send()

            @pl.when((b >= z) & (z > 0))
            def _():
                down(b, c).wait_send()


def pick_kernel(owner_ref, block_ref, out_ref):
    out_ref[...] = block_ref[...]


def gathered(n, reps, amplitudes, amp_mask, integrals, int_mask, owner_map):
    rows, depth = amplitudes.shape
    wide = integrals.shape[1]
    width = wide // reps
    steps = owner_map.shape[0]
    dma = pltpu.SemaphoreType.DMA
    bf16 = jnp.bfloat16
    by_owner = pl.pallas_call(
        functools.partial(gather_kernel, n, reps),
        out_shape=jax.ShapeDtypeStruct((n, rows, width), bf16),
        in_specs=[pl.BlockSpec(memory_space=pltpu.SMEM)] * 2 + [pl.BlockSpec(memory_space=pl.ANY)] * 2,
        out_specs=pl.BlockSpec(memory_space=pltpu.VMEM),
        scratch_shapes=[
            pltpu.VMEM((n, rows, depth), bf16),
            pltpu.VMEM((depth, wide), bf16),
            pltpu.VMEM((n, rows, width), bf16),
            pltpu.VMEM((reps - 1, n, rows, width), bf16),
            pltpu.VMEM((reps - 1, n, rows, width), bf16),
            dma((2,)),
            dma((n, CHUNKS)), dma((n, CHUNKS)), dma((n, CHUNKS)), dma((n, CHUNKS)),
            dma((reps - 1, n, CHUNKS)), dma((reps - 1, n, CHUNKS)),
        ],
        compiler_params=pltpu.CompilerParams(
            collective_id=0, has_side_effects=True, vmem_limit_bytes=40 * 1024 * 1024),
        cost_estimate=pl.CostEstimate(
            flops=2 * n * rows * depth * wide, bytes_accessed=2 * (rows * depth + depth * wide + n * rows * width),
            transcendentals=0),
    )(amp_mask, int_mask, amplitudes, integrals)
    return pl.pallas_call(
        pick_kernel,
        out_shape=jax.ShapeDtypeStruct((steps, rows, width), bf16),
        grid_spec=pltpu.PrefetchScalarGridSpec(
            num_scalar_prefetch=1,
            grid=(steps,),
            in_specs=[pl.BlockSpec((1, rows, width), lambda s, owner: (owner[s], 0, 0))],
            out_specs=pl.BlockSpec((1, rows, width), lambda s, owner: (s, 0, 0)),
        ),
    )(owner_map, by_owner)


def solution(mesh):
    n, reps = mesh.shape["tile"], mesh.shape["rep"]

    def shards(amplitudes, amp_mask, integrals, int_mask, owner_map):
        if n > owner_map.shape[0]:
            return stepwise(amplitudes, amp_mask, integrals, int_mask, owner_map)
        return gathered(n, reps, amplitudes, amp_mask, integrals, int_mask, owner_map)

    placed = (
        P(("groups", "tile", "sub"), "rep"),
        P(("groups", "tile", "sub"), "rep"),
        P("rep", "tile"),
        P("rep", "tile"),
        P("groups"),
    )
    return jax.shard_map(
        shards,
        mesh=mesh,
        in_specs=placed,
        out_specs=P("groups", "sub", ("tile", "rep")),
        check_vma=False,
    )
```

```python
import functools

import jax
import jax.numpy as jnp
from jax import lax
from jax.experimental import pallas as pl
from jax.experimental.pallas import tpu as pltpu
from jax.sharding import PartitionSpec as P

TILE = 128
CHUNKS = 4
MESH = pl.DeviceIdType.MESH


def expand_mask(mask):
    big = jnp.repeat(jnp.repeat(mask, TILE, axis=0), TILE, axis=1)
    return big.astype(jnp.bfloat16)


def from_root(block, axis, source):
    block = jnp.where(lax.axis_index(axis) == source, block, jnp.zeros_like(block))
    return lax.psum(block, axis)


def stepwise(amplitudes, amp_mask, integrals, int_mask, owner_map):
    masked_amp = amplitudes * expand_mask(amp_mask)
    masked_int = integrals * expand_mask(int_mask)
    results = []
    for step in range(owner_map.shape[0]):
        block_rows = from_root(masked_amp, "tile", owner_map[step])
        partial_value = jnp.dot(block_rows, masked_int, preferred_element_type=jnp.float32)
        summed = lax.psum_scatter(
            partial_value.astype(jnp.bfloat16), "rep", scatter_dimension=1, tiled=True
        )
        results.append(summed)
    return jnp.stack(results, axis=0)


def tile_scale(mask_ref, i, j, shape):
    return jnp.full(shape, mask_ref[i, j].astype(jnp.float32), jnp.float32).astype(jnp.bfloat16)


def gather_kernel(
    n, reps, owner_hbm, amp_mask_hbm, int_mask_hbm, amp_hbm, int_hbm, out_ref,
    owner, amp_mask, int_mask, blocks, ints, mine, sent, got,
    load_sem, up_send, up_recv, down_send, down_recv, x_send, x_recv,
):
    z = lax.axis_index("tile")
    x = lax.axis_index("rep")
    rows, depth = amp_hbm.shape
    part = rows // CHUNKS
    width = int_hbm.shape[1] // reps

    loads = [
        pltpu.make_async_copy(source, target, load_sem.at[2 + at])
        for at, (source, target) in enumerate(
            ((amp_mask_hbm, amp_mask), (int_mask_hbm, int_mask), (owner_hbm, owner)))
    ]
    for load in loads:
        load.start()
    load_amp = pltpu.make_async_copy(amp_hbm, blocks.at[z], load_sem.at[0])
    load_int = pltpu.make_async_copy(int_hbm, ints, load_sem.at[1])
    load_amp.start()
    load_int.start()

    barrier = pltpu.get_barrier_semaphore()

    @pl.when(z > 0)
    def _():
        pl.semaphore_signal(barrier, inc=1, device_id={"tile": z - 1}, device_id_type=MESH)

    @pl.when(z < n - 1)
    def _():
        pl.semaphore_signal(barrier, inc=1, device_id={"tile": z + 1}, device_id_type=MESH)

    for k in range(1, reps):
        pl.semaphore_signal(barrier, inc=1, device_id={"rep": lax.rem(x + k, reps)}, device_id_type=MESH)
    pl.semaphore_wait(barrier, jnp.where(z > 0, 1, 0) + jnp.where(z < n - 1, 1, 0) + (reps - 1))

    def span(c):
        return pl.ds(pl.multiple_of(c * part, part), part)

    def up(b, c):
        piece = blocks.at[b, span(c)]
        return pltpu.make_async_remote_copy(
            src_ref=piece, dst_ref=piece, send_sem=up_send.at[b, c], recv_sem=up_recv.at[b, c],
            device_id={"tile": z + 1}, device_id_type=MESH)

    def down(b, c):
        piece = blocks.at[b, span(c)]
        return pltpu.make_async_remote_copy(
            src_ref=piece, dst_ref=piece, send_sem=down_send.at[b, c], recv_sem=down_recv.at[b, c],
            device_id={"tile": z - 1}, device_id_type=MESH)

    def across(k, b, c):
        return pltpu.make_async_remote_copy(
            src_ref=sent.at[k - 1, b, span(c)], dst_ref=got.at[k - 1, b, span(c)],
            send_sem=x_send.at[k - 1, b, c], recv_sem=x_recv.at[k - 1, b, c],
            device_id={"rep": lax.rem(x + k, reps)}, device_id_type=MESH)

    def columns(r):
        return pl.ds(pl.multiple_of(r * width, width), width)

    def compute(b, c):
        for k in range(1, reps):
            sent[k - 1, b, span(c), :] = jnp.dot(
                blocks[b, span(c), :], ints[:, columns(lax.rem(x + k, reps))],
                preferred_element_type=jnp.float32).astype(jnp.bfloat16)
            across(k, b, c).start()
        mine[b, span(c), :] = jnp.dot(
            blocks[b, span(c), :], ints[:, columns(x)],
            preferred_element_type=jnp.float32).astype(jnp.bfloat16)

    def finish(b, c):
        total = mine[b, span(c), :].astype(jnp.float32)
        for k in range(1, reps):
            across(k, b, c).wait_recv()
            total = total + got[k - 1, b, span(c), :].astype(jnp.float32)
        mine[b, span(c), :] = total.astype(jnp.bfloat16)

    for load in loads:
        load.wait()
    load_amp.wait()
    for c in range(CHUNKS):
        at = slice(c * part, (c + 1) * part)
        for j in range(depth // TILE):
            here = slice(j * TILE, (j + 1) * TILE)
            scale = tile_scale(amp_mask, c * part // TILE, j, (part, TILE))
            blocks[z, at, here] = blocks[z, at, here] * scale

        @pl.when(z < n - 1)
        def _():
            up(z, c).start()

        @pl.when(z > 0)
        def _():
            down(z, c).start()

    load_int.wait()
    for j in range(int_hbm.shape[1] // TILE):
        here = slice(j * TILE, (j + 1) * TILE)

        @pl.loop(0, depth // TILE)
        def _(i):
            at = pl.ds(pl.multiple_of(i * TILE, TILE), TILE)
            ints[at, here] = ints[at, here] * tile_scale(int_mask, i, j, (TILE, TILE))

    @pl.loop(0, CHUNKS)
    def _(c):
        compute(z, c)

    @pl.loop(1, n)
    def _(d):
        lower, upper = z - d, z + d

        @pl.loop(0, CHUNKS)
        def _(c):
            @pl.when(lower >= 0)
            def _():
                up(lower, c).wait_recv()

                @pl.when(z < n - 1)
                def _():
                    up(lower, c).start()

            @pl.when(upper < n)
            def _():
                down(upper, c).wait_recv()

                @pl.when(z > 0)
                def _():
                    down(upper, c).start()

            @pl.when(lower >= 0)
            def _():
                compute(lower, c)

            @pl.when(upper < n)
            def _():
                compute(upper, c)

            @pl.when(lower + 1 >= 0)
            def _():
                finish(lower + 1, c)

            @pl.when((upper - 1 < n) & (d > 1))
            def _():
                finish(upper - 1, c)

    @pl.loop(0, CHUNKS)
    def _(c):
        @pl.when(z == n - 1)
        def _():
            finish(0, c)

        @pl.when(z == 0)
        def _():
            finish(n - 1, c)

    for step in range(out_ref.shape[0]):
        out_ref[step] = mine[owner[step]]

    @pl.loop(0, n)
    def _(b):
        @pl.loop(0, CHUNKS)
        def _(c):
            for k in range(1, reps):
                across(k, b, c).wait_send()

            @pl.when((b <= z) & (z < n - 1))
            def _():
                up(b, c).wait_send()

            @pl.when((b >= z) & (z > 0))
            def _():
                down(b, c).wait_send()


def gathered(n, reps, amplitudes, amp_mask, integrals, int_mask, owner_map):
    rows, depth = amplitudes.shape
    wide = integrals.shape[1]
    width = wide // reps
    steps = owner_map.shape[0]
    dma = pltpu.SemaphoreType.DMA
    bf16 = jnp.bfloat16
    return pl.pallas_call(
        functools.partial(gather_kernel, n, reps),
        out_shape=jax.ShapeDtypeStruct((steps, rows, width), bf16),
        in_specs=[pl.BlockSpec(memory_space=pl.ANY)] * 5,
        out_specs=pl.BlockSpec(memory_space=pltpu.VMEM),
        scratch_shapes=[
            pltpu.SMEM(owner_map.shape, jnp.int32),
            pltpu.SMEM(amp_mask.shape, jnp.int32),
            pltpu.SMEM(int_mask.shape, jnp.int32),
            pltpu.VMEM((n, rows, depth), bf16),
            pltpu.VMEM((depth, wide), bf16),
            pltpu.VMEM((n, rows, width), bf16),
            pltpu.VMEM((reps - 1, n, rows, width), bf16),
            pltpu.VMEM((reps - 1, n, rows, width), bf16),
            dma((5,)),
            dma((n, CHUNKS)), dma((n, CHUNKS)), dma((n, CHUNKS)), dma((n, CHUNKS)),
            dma((reps - 1, n, CHUNKS)), dma((reps - 1, n, CHUNKS)),
        ],
        compiler_params=pltpu.CompilerParams(
            collective_id=0, has_side_effects=True, vmem_limit_bytes=62 * 1024 * 1024),
        cost_estimate=pl.CostEstimate(
            flops=2 * n * rows * depth * wide, bytes_accessed=2 * (rows * depth + depth * wide + n * rows * width),
            transcendentals=0),
    )(owner_map, amp_mask, int_mask, amplitudes, integrals)


def solution(mesh):
    n, reps = mesh.shape["tile"], mesh.shape["rep"]

    def shards(amplitudes, amp_mask, integrals, int_mask, owner_map):
        if n > owner_map.shape[0]:
            return stepwise(amplitudes, amp_mask, integrals, int_mask, owner_map)
        return gathered(n, reps, amplitudes, amp_mask, integrals, int_mask, owner_map)

    placed = (
        P(("groups", "tile", "sub"), "rep"),
        P(("groups", "tile", "sub"), "rep"),
        P("rep", "tile"),
        P("rep", "tile"),
        P("groups"),
    )
    return jax.shard_map(
        shards,
        mesh=mesh,
        in_specs=placed,
        out_specs=P("groups", "sub", ("tile", "rep")),
        check_vma=False,
    )
```

```python
import functools

import jax
import jax.numpy as jnp
from jax import lax
from jax.experimental import pallas as pl
from jax.experimental.pallas import tpu as pltpu
from jax.sharding import PartitionSpec as P

TILE = 128
CHUNKS = 4
MESH = pl.DeviceIdType.MESH


def expand_mask(mask):
    big = jnp.repeat(jnp.repeat(mask, TILE, axis=0), TILE, axis=1)
    return big.astype(jnp.bfloat16)


def from_root(block, axis, source):
    block = jnp.where(lax.axis_index(axis) == source, block, jnp.zeros_like(block))
    return lax.psum(block, axis)


def stepwise(amplitudes, amp_mask, integrals, int_mask, owner_map):
    masked_amp = amplitudes * expand_mask(amp_mask)
    masked_int = integrals * expand_mask(int_mask)
    results = []
    for step in range(owner_map.shape[0]):
        block_rows = from_root(masked_amp, "tile", owner_map[step])
        partial_value = jnp.dot(block_rows, masked_int, preferred_element_type=jnp.float32)
        summed = lax.psum_scatter(
            partial_value.astype(jnp.bfloat16), "rep", scatter_dimension=1, tiled=True
        )
        results.append(summed)
    return jnp.stack(results, axis=0)


def tile_scale(mask_ref, i, j, shape):
    return jnp.full(shape, mask_ref[i, j].astype(jnp.float32), jnp.float32).astype(jnp.bfloat16)


def gather_kernel(
    n, reps, owner_hbm, amp_mask_hbm, int_mask_hbm, amp_hbm, int_hbm, out_ref,
    owner, amp_mask, int_mask, blocks, ints, mine, sent, got,
    load_sem, up_send, up_recv, down_send, down_recv, x_send, x_recv,
):
    z = lax.axis_index("tile")
    x = lax.axis_index("rep")
    rows, depth = amp_hbm.shape
    part = rows // CHUNKS
    width = int_hbm.shape[1] // reps

    loads = [
        pltpu.make_async_copy(source, target, load_sem.at[2 + at])
        for at, (source, target) in enumerate(
            ((amp_mask_hbm, amp_mask), (int_mask_hbm, int_mask), (owner_hbm, owner)))
    ]
    for load in loads:
        load.start()
    load_amp = pltpu.make_async_copy(amp_hbm, blocks.at[z], load_sem.at[0])
    load_int = pltpu.make_async_copy(int_hbm, ints, load_sem.at[1])
    load_amp.start()
    load_int.start()

    barrier = pltpu.get_barrier_semaphore()

    @pl.when(z > 0)
    def _():
        pl.semaphore_signal(barrier, inc=1, device_id={"tile": z - 1}, device_id_type=MESH)

    @pl.when(z < n - 1)
    def _():
        pl.semaphore_signal(barrier, inc=1, device_id={"tile": z + 1}, device_id_type=MESH)

    for k in range(1, reps):
        pl.semaphore_signal(barrier, inc=1, device_id={"rep": lax.rem(x + k, reps)}, device_id_type=MESH)
    pl.semaphore_wait(barrier, jnp.where(z > 0, 1, 0) + jnp.where(z < n - 1, 1, 0) + (reps - 1))

    def span(c):
        return pl.ds(pl.multiple_of(c * part, part), part)

    def up(b, c):
        piece = blocks.at[b, span(c)]
        return pltpu.make_async_remote_copy(
            src_ref=piece, dst_ref=piece, send_sem=up_send.at[b, c], recv_sem=up_recv.at[b, c],
            device_id={"tile": z + 1}, device_id_type=MESH)

    def down(b, c):
        piece = blocks.at[b, span(c)]
        return pltpu.make_async_remote_copy(
            src_ref=piece, dst_ref=piece, send_sem=down_send.at[b, c], recv_sem=down_recv.at[b, c],
            device_id={"tile": z - 1}, device_id_type=MESH)

    def across(k, b, c):
        return pltpu.make_async_remote_copy(
            src_ref=sent.at[k - 1, b, span(c)], dst_ref=got.at[k - 1, b, span(c)],
            send_sem=x_send.at[k - 1, b, c], recv_sem=x_recv.at[k - 1, b, c],
            device_id={"rep": lax.rem(x + k, reps)}, device_id_type=MESH)

    def columns(r):
        return pl.ds(pl.multiple_of(r * width, width), width)

    def compute(b, c):
        for k in range(1, reps):
            sent[k - 1, b, span(c), :] = jnp.dot(
                blocks[b, span(c), :], ints[:, columns(lax.rem(x + k, reps))],
                preferred_element_type=jnp.float32).astype(jnp.bfloat16)
            across(k, b, c).start()
        mine[b, span(c), :] = jnp.dot(
            blocks[b, span(c), :], ints[:, columns(x)],
            preferred_element_type=jnp.float32).astype(jnp.bfloat16)

    def finish(b, c):
        total = mine[b, span(c), :].astype(jnp.float32)
        for k in range(1, reps):
            across(k, b, c).wait_recv()
            total = total + got[k - 1, b, span(c), :].astype(jnp.float32)
        mine[b, span(c), :] = total.astype(jnp.bfloat16)

    for load in loads:
        load.wait()
    load_amp.wait()
    for c in range(CHUNKS):
        at = slice(c * part, (c + 1) * part)
        for j in range(depth // TILE):
            here = slice(j * TILE, (j + 1) * TILE)
            scale = tile_scale(amp_mask, c * part // TILE, j, (part, TILE))
            blocks[z, at, here] = blocks[z, at, here] * scale

        @pl.when(z < n - 1)
        def _():
            up(z, c).start()

        @pl.when(z > 0)
        def _():
            down(z, c).start()

    load_int.wait()
    for j in range(int_hbm.shape[1] // TILE):
        here = slice(j * TILE, (j + 1) * TILE)

        @pl.loop(0, depth // TILE)
        def _(i):
            at = pl.ds(pl.multiple_of(i * TILE, TILE), TILE)
            ints[at, here] = ints[at, here] * tile_scale(int_mask, i, j, (TILE, TILE))

    @pl.loop(0, CHUNKS)
    def _(c):
        compute(z, c)

    @pl.loop(1, n)
    def _(d):
        lower, upper = z - d, z + d

        @pl.loop(0, CHUNKS)
        def _(c):
            @pl.when(lower >= 0)
            def _():
                up(lower, c).wait_recv()

                @pl.when(z < n - 1)
                def _():
                    up(lower, c).start()

            @pl.when(upper < n)
            def _():
                down(upper, c).wait_recv()

                @pl.when(z > 0)
                def _():
                    down(upper, c).start()

            @pl.when(lower >= 0)
            def _():
                compute(lower, c)

            @pl.when(upper < n)
            def _():
                compute(upper, c)

            @pl.when(lower + 1 >= 0)
            def _():
                finish(lower + 1, c)

            @pl.when((upper - 1 < n) & (d > 1))
            def _():
                finish(upper - 1, c)

    @pl.loop(0, CHUNKS)
    def _(c):
        @pl.when(z == n - 1)
        def _():
            finish(0, c)

        @pl.when(z == 0)
        def _():
            finish(n - 1, c)

    for step in range(out_ref.shape[0]):
        out_ref[step] = mine[owner[step]]

    @pl.loop(0, n)
    def _(b):
        @pl.loop(0, CHUNKS)
        def _(c):
            for k in range(1, reps):
                across(k, b, c).wait_send()

            @pl.when((b <= z) & (z < n - 1))
            def _():
                up(b, c).wait_send()

            @pl.when((b >= z) & (z > 0))
            def _():
                down(b, c).wait_send()


def gathered(n, reps, amplitudes, amp_mask, integrals, int_mask, owner_map):
    rows, depth = amplitudes.shape
    wide = integrals.shape[1]
    width = wide // reps
    steps = owner_map.shape[0]
    dma = pltpu.SemaphoreType.DMA
    bf16 = jnp.bfloat16
    return pl.pallas_call(
        functools.partial(gather_kernel, n, reps),
        out_shape=jax.ShapeDtypeStruct((steps, rows, width), bf16),
        in_specs=[pl.BlockSpec(memory_space=pl.ANY)] * 5,
        out_specs=pl.BlockSpec(memory_space=pltpu.VMEM),
        scratch_shapes=[
            pltpu.SMEM(owner_map.shape, jnp.int32),
            pltpu.SMEM(amp_mask.shape, jnp.int32),
            pltpu.SMEM(int_mask.shape, jnp.int32),
            pltpu.VMEM((n, rows, depth), bf16),
            pltpu.VMEM((depth, wide), bf16),
            pltpu.VMEM((n, rows, width), bf16),
            pltpu.VMEM((reps - 1, n, rows, width), bf16),
            pltpu.VMEM((reps - 1, n, rows, width), bf16),
            dma((5,)),
            dma((n, CHUNKS)), dma((n, CHUNKS)), dma((n, CHUNKS)), dma((n, CHUNKS)),
            dma((reps - 1, n, CHUNKS)), dma((reps - 1, n, CHUNKS)),
        ],
        compiler_params=pltpu.CompilerParams(
            collective_id=0, has_side_effects=True, vmem_limit_bytes=24 * 1024 * 1024),
        cost_estimate=pl.CostEstimate(
            flops=2 * n * rows * depth * wide, bytes_accessed=2 * (rows * depth + depth * wide + n * rows * width),
            transcendentals=0),
    )(*(pltpu.with_memory_space_constraint(each, pltpu.HBM)
        for each in (owner_map, amp_mask, int_mask, amplitudes, integrals)))


def solution(mesh):
    n, reps = mesh.shape["tile"], mesh.shape["rep"]

    def shards(amplitudes, amp_mask, integrals, int_mask, owner_map):
        if n > owner_map.shape[0]:
            return stepwise(amplitudes, amp_mask, integrals, int_mask, owner_map)
        return gathered(n, reps, amplitudes, amp_mask, integrals, int_mask, owner_map)

    placed = (
        P(("groups", "tile", "sub"), "rep"),
        P(("groups", "tile", "sub"), "rep"),
        P("rep", "tile"),
        P("rep", "tile"),
        P("groups"),
    )
    return jax.shard_map(
        shards,
        mesh=mesh,
        in_specs=placed,
        out_specs=P("groups", "sub", ("tile", "rep")),
        check_vma=False,
    )
```

```python
import functools

import jax
import jax.numpy as jnp
from jax import lax
from jax.experimental import pallas as pl
from jax.experimental.pallas import tpu as pltpu
from jax.sharding import PartitionSpec as P

TILE = 128
CHUNKS = 4
MESH = pl.DeviceIdType.MESH


def expand_mask(mask):
    big = jnp.repeat(jnp.repeat(mask, TILE, axis=0), TILE, axis=1)
    return big.astype(jnp.bfloat16)


def from_root(block, axis, source):
    block = jnp.where(lax.axis_index(axis) == source, block, jnp.zeros_like(block))
    return lax.psum(block, axis)


def stepwise(amplitudes, amp_mask, integrals, int_mask, owner_map):
    masked_amp = amplitudes * expand_mask(amp_mask)
    masked_int = integrals * expand_mask(int_mask)
    results = []
    for step in range(owner_map.shape[0]):
        block_rows = from_root(masked_amp, "tile", owner_map[step])
        partial_value = jnp.dot(block_rows, masked_int, preferred_element_type=jnp.float32)
        summed = lax.psum_scatter(
            partial_value.astype(jnp.bfloat16), "rep", scatter_dimension=1, tiled=True
        )
        results.append(summed)
    return jnp.stack(results, axis=0)


def tile_scale(mask_ref, i, j, shape):
    return jnp.full(shape, mask_ref[i, j].astype(jnp.float32), jnp.float32).astype(jnp.bfloat16)


def gather_kernel(
    n, reps, owner_hbm, amp_mask_hbm, int_mask_hbm, amp_hbm, int_hbm, out_ref,
    owner, amp_mask, int_mask, blocks, ints, mine, sent, got, end_ints, help_mine, help_sent, help_got,
    load_sem, up_send, up_recv, down_send, down_recv, x_send, x_recv,
    int_send, int_recv, y_send, y_recv, sub_send, sub_recv, help_send, help_recv, back_send, back_recv,
):
    z = lax.axis_index("tile")
    x = lax.axis_index("rep")
    rows, depth = amp_hbm.shape
    part = rows // CHUNKS
    width = int_hbm.shape[1] // reps
    group, sub = lax.axis_index("groups"), lax.axis_index("sub")
    is_end = (z == 0) | (z == n - 1)
    is_helper = (z == 1) | (z == n - 2)
    helper = jnp.where(z == 0, 1, n - 2)
    end = jnp.where(z == 1, 0, n - 1)
    quarter = depth // 4
    slab = quarter // CHUNKS

    loads = [
        pltpu.make_async_copy(source, target, load_sem.at[2 + at])
        for at, (source, target) in enumerate(
            ((amp_mask_hbm, amp_mask), (int_mask_hbm, int_mask), (owner_hbm, owner)))
    ]
    for load in loads:
        load.start()
    load_amp = pltpu.make_async_copy(amp_hbm, blocks.at[z], load_sem.at[0])
    load_int = pltpu.make_async_copy(int_hbm, ints, load_sem.at[1])
    load_amp.start()
    load_int.start()

    barrier = pltpu.get_barrier_semaphore()

    @pl.when(z > 0)
    def _():
        pl.semaphore_signal(barrier, inc=1, device_id={"tile": z - 1}, device_id_type=MESH)

    @pl.when(z < n - 1)
    def _():
        pl.semaphore_signal(barrier, inc=1, device_id={"tile": z + 1}, device_id_type=MESH)

    for k in range(1, reps):
        pl.semaphore_signal(barrier, inc=1, device_id={"rep": lax.rem(x + k, reps)}, device_id_type=MESH)

    @pl.when(is_helper)
    def _():
        pl.semaphore_signal(barrier, inc=1, device_id={"groups": 1 - group}, device_id_type=MESH)
        pl.semaphore_signal(barrier, inc=1, device_id={"sub": 1 - sub}, device_id_type=MESH)

    pl.semaphore_wait(barrier, jnp.where(is_helper, 2, 0) + jnp.where(z > 0, 1, 0) + jnp.where(z < n - 1, 1, 0) + (reps - 1))

    def span(c):
        return pl.ds(pl.multiple_of(c * part, part), part)

    def up(b, c):
        piece = blocks.at[b, span(c)]
        return pltpu.make_async_remote_copy(
            src_ref=piece, dst_ref=piece, send_sem=up_send.at[b, c], recv_sem=up_recv.at[b, c],
            device_id={"tile": z + 1}, device_id_type=MESH)

    def down(b, c):
        piece = blocks.at[b, span(c)]
        return pltpu.make_async_remote_copy(
            src_ref=piece, dst_ref=piece, send_sem=down_send.at[b, c], recv_sem=down_recv.at[b, c],
            device_id={"tile": z - 1}, device_id_type=MESH)

    def across(k, b, c):
        return pltpu.make_async_remote_copy(
            src_ref=sent.at[k - 1, b, span(c)], dst_ref=got.at[k - 1, b, span(c)],
            send_sem=x_send.at[k - 1, b, c], recv_sem=x_recv.at[k - 1, b, c],
            device_id={"rep": lax.rem(x + k, reps)}, device_id_type=MESH)

    def slab_of(g, u, c):
        return pl.ds(pl.multiple_of((g * 2 + u) * quarter + c * slab, slab), slab)

    def to_helper(c):
        return pltpu.make_async_remote_copy(
            src_ref=ints.at[slab_of(group, sub, c)], dst_ref=end_ints.at[slab_of(group, sub, c)],
            send_sem=int_send.at[c], recv_sem=int_recv.at[c], device_id={"tile": helper}, device_id_type=MESH)

    def from_end(c):
        piece = end_ints.at[slab_of(group, sub, c)]
        return pltpu.make_async_remote_copy(
            src_ref=piece, dst_ref=piece,
            send_sem=int_send.at[c], recv_sem=int_recv.at[c], device_id={"tile": end}, device_id_type=MESH)

    def over_y(g, c):
        piece = end_ints.at[slab_of(g, sub, c)]
        return pltpu.make_async_remote_copy(
            src_ref=piece, dst_ref=piece, send_sem=y_send.at[c], recv_sem=y_recv.at[c],
            device_id={"groups": 1 - group}, device_id_type=MESH)

    def over_sub(k, u, c):
        piece = end_ints.at[slab_of(group if k == 0 else 1 - group, u, c)]
        return pltpu.make_async_remote_copy(
            src_ref=piece, dst_ref=piece, send_sem=sub_send.at[k, c], recv_sem=sub_recv.at[k, c],
            device_id={"sub": 1 - sub}, device_id_type=MESH)

    def help_across(c):
        return pltpu.make_async_remote_copy(
            src_ref=help_sent.at[span(c)], dst_ref=help_got.at[span(c)],
            send_sem=help_send.at[c], recv_sem=help_recv.at[c],
            device_id={"rep": 1 - x}, device_id_type=MESH)

    def back(b, to, c):
        return pltpu.make_async_remote_copy(
            src_ref=help_mine.at[span(c)], dst_ref=mine.at[b, span(c)],
            send_sem=back_send.at[c], recv_sem=back_recv.at[c],
            device_id={"tile": to}, device_id_type=MESH)

    def pass_on(c):
        over_y(1 - group, c).wait_recv()
        over_sub(1, sub, c).start()

    def help_compute(c):
        help_sent[span(c), :] = jnp.dot(
            blocks[z, span(c), :], end_ints[:, columns(1 - x)],
            preferred_element_type=jnp.float32).astype(jnp.bfloat16)
        help_across(c).start()
        help_mine[span(c), :] = jnp.dot(
            blocks[z, span(c), :], end_ints[:, columns(x)],
            preferred_element_type=jnp.float32).astype(jnp.bfloat16)

    def help_finish(c):
        help_across(c).wait_recv()
        total = help_mine[span(c), :].astype(jnp.float32) + help_got[span(c), :].astype(jnp.float32)
        help_mine[span(c), :] = total.astype(jnp.bfloat16)
        back(z, end, c).start()

    def mask_ints(i):
        for j in range(int_hbm.shape[1] // TILE):
            at = pl.ds(pl.multiple_of(i * TILE, TILE), TILE)
            here = slice(j * TILE, (j + 1) * TILE)
            ints[at, here] = ints[at, here] * tile_scale(int_mask, i, j, (TILE, TILE))

    def columns(r):
        return pl.ds(pl.multiple_of(r * width, width), width)

    def compute(b, c):
        for k in range(1, reps):
            sent[k - 1, b, span(c), :] = jnp.dot(
                blocks[b, span(c), :], ints[:, columns(lax.rem(x + k, reps))],
                preferred_element_type=jnp.float32).astype(jnp.bfloat16)
            across(k, b, c).start()
        mine[b, span(c), :] = jnp.dot(
            blocks[b, span(c), :], ints[:, columns(x)],
            preferred_element_type=jnp.float32).astype(jnp.bfloat16)

    def finish(b, c):
        total = mine[b, span(c), :].astype(jnp.float32)
        for k in range(1, reps):
            across(k, b, c).wait_recv()
            total = total + got[k - 1, b, span(c), :].astype(jnp.float32)
        mine[b, span(c), :] = total.astype(jnp.bfloat16)

    for load in loads:
        load.wait()

    tall = depth // TILE
    first = (group * 2 + sub) * (quarter // TILE)

    @pl.when(is_end)
    def _():
        load_int.wait()

        @pl.loop(0, quarter // TILE)
        def _(i):
            mask_ints(first + i)

        for c in range(CHUNKS):
            to_helper(c).start()

    load_amp.wait()
    for c in range(CHUNKS):
        at = slice(c * part, (c + 1) * part)
        for j in range(depth // TILE):
            here = slice(j * TILE, (j + 1) * TILE)
            scale = tile_scale(amp_mask, c * part // TILE, j, (part, TILE))
            blocks[z, at, here] = blocks[z, at, here] * scale

        @pl.when(z < n - 2)
        def _():
            up(z, c).start()

        @pl.when(z > 1)
        def _():
            down(z, c).start()

    @pl.when(jnp.logical_not(is_end))
    def _():
        load_int.wait()

        @pl.loop(0, quarter // TILE)
        def _(i):
            mask_ints(first + i)

    @pl.loop(quarter // TILE, tall)
    def _(i):
        mask_ints(lax.rem(first + i, tall))

    @pl.loop(0, CHUNKS)
    def _(c):
        compute(z, c)

    w = n - 1 - z

    def comes(far, d):
        near = (d == 1) & (far > 1) & (far < n - 1)
        return near | ((d > 1) & (far - d >= 0)) | ((d == 2) & (far == 1))

    def lower(d):
        return jnp.maximum(z - d, 0)

    def upper(d):
        return n - 1 - jnp.maximum(w - d, 0)

    def finish_all(d, c):
        @pl.when(d == 0)
        def _():
            finish(z, c)

        @pl.when(comes(z, d))
        def _():
            finish(lower(d), c)

        @pl.when(comes(w, d))
        def _():
            finish(upper(d), c)

    @pl.loop(1, n)
    def _(d):
        @pl.loop(0, CHUNKS)
        def _(c):
            @pl.when(is_helper & (d == 1))
            def _():
                from_end(c).wait_recv()
                over_y(group, c).start()
                over_sub(0, sub, c).start()

            @pl.when(comes(z, d))
            def _():
                up(lower(d), c).wait_recv()

                @pl.when(z < n - 1)
                def _():
                    up(lower(d), c).start()

            @pl.when(comes(w, d))
            def _():
                down(upper(d), c).wait_recv()

                @pl.when(z > 0)
                def _():
                    down(upper(d), c).start()

            @pl.when(is_helper & (d == 1) & (c > 0))
            def _():
                pass_on(c - 1)

            @pl.when(comes(z, d))
            def _():
                compute(lower(d), c)

            @pl.when(comes(w, d))
            def _():
                compute(upper(d), c)

            @pl.when(is_helper & (d == 2))
            def _():
                @pl.when(c == 0)
                def _():
                    for piece in range(CHUNKS):
                        over_sub(0, 1 - sub, piece).wait_recv()
                        over_sub(1, 1 - sub, piece).wait_recv()

                help_compute(c)

                @pl.when(c > 0)
                def _():
                    help_finish(c - 1)

            finish_all(d - 1, c)

        @pl.when(is_helper & (d == 1))
        def _():
            pass_on(CHUNKS - 1)

        @pl.when(is_helper & (d == 2))
        def _():
            help_finish(CHUNKS - 1)

    @pl.loop(0, CHUNKS)
    def _(c):
        finish_all(n - 1, c)

        @pl.when(is_end)
        def _():
            back(helper, helper, c).wait_recv()

    for step in range(out_ref.shape[0]):
        out_ref[step] = mine[owner[step]]

    @pl.loop(0, n)
    def _(b):
        @pl.loop(0, CHUNKS)
        def _(c):
            @pl.when(jnp.logical_not(is_end & (b == helper)))
            def _():
                for k in range(1, reps):
                    across(k, b, c).wait_send()

            @pl.when((b <= z) & (z < n - 1) & (b != n - 2))
            def _():
                up(b, c).wait_send()

            @pl.when((b >= z) & (z > 0) & (b != 1))
            def _():
                down(b, c).wait_send()

    @pl.loop(0, CHUNKS)
    def _(c):
        @pl.when(is_end)
        def _():
            to_helper(c).wait_send()

        @pl.when(is_helper)
        def _():
            over_y(group, c).wait_send()
            over_sub(0, sub, c).wait_send()
            over_sub(1, sub, c).wait_send()
            help_across(c).wait_send()
            back(z, end, c).wait_send()


def gathered(n, reps, amplitudes, amp_mask, integrals, int_mask, owner_map):
    rows, depth = amplitudes.shape
    wide = integrals.shape[1]
    width = wide // reps
    steps = owner_map.shape[0]
    dma = pltpu.SemaphoreType.DMA
    bf16 = jnp.bfloat16
    return pl.pallas_call(
        functools.partial(gather_kernel, n, reps),
        out_shape=jax.ShapeDtypeStruct((steps, rows, width), bf16),
        in_specs=[pl.BlockSpec(memory_space=pl.ANY)] * 5,
        out_specs=pl.BlockSpec(memory_space=pltpu.VMEM),
        scratch_shapes=[
            pltpu.SMEM(owner_map.shape, jnp.int32),
            pltpu.SMEM(amp_mask.shape, jnp.int32),
            pltpu.SMEM(int_mask.shape, jnp.int32),
            pltpu.VMEM((n, rows, depth), bf16),
            pltpu.VMEM((depth, wide), bf16),
            pltpu.VMEM((n, rows, width), bf16),
            pltpu.VMEM((reps - 1, n, rows, width), bf16),
            pltpu.VMEM((reps - 1, n, rows, width), bf16),
            pltpu.VMEM((depth, wide), bf16),
            pltpu.VMEM((rows, width), bf16),
            pltpu.VMEM((rows, width), bf16),
            pltpu.VMEM((rows, width), bf16),
            dma((5,)),
            dma((n, CHUNKS)), dma((n, CHUNKS)), dma((n, CHUNKS)), dma((n, CHUNKS)),
            dma((reps - 1, n, CHUNKS)), dma((reps - 1, n, CHUNKS)),
            dma((CHUNKS,)), dma((CHUNKS,)), dma((CHUNKS,)), dma((CHUNKS,)),
            dma((2, CHUNKS)), dma((2, CHUNKS)),
            dma((CHUNKS,)), dma((CHUNKS,)), dma((CHUNKS,)), dma((CHUNKS,)),
        ],
        compiler_params=pltpu.CompilerParams(
            collective_id=0, has_side_effects=True, vmem_limit_bytes=24 * 1024 * 1024),
        cost_estimate=pl.CostEstimate(
            flops=2 * n * rows * depth * wide, bytes_accessed=2 * (rows * depth + depth * wide + n * rows * width),
            transcendentals=0),
    )(*(pltpu.with_memory_space_constraint(each, pltpu.HBM)
        for each in (owner_map, amp_mask, int_mask, amplitudes, integrals)))


def solution(mesh):
    n, reps = mesh.shape["tile"], mesh.shape["rep"]
    pairs = mesh.shape["groups"] == mesh.shape["sub"] == reps == 2

    def shards(amplitudes, amp_mask, integrals, int_mask, owner_map):
        if n > owner_map.shape[0] or n != 4 or not pairs:
            return stepwise(amplitudes, amp_mask, integrals, int_mask, owner_map)
        return gathered(n, reps, amplitudes, amp_mask, integrals, int_mask, owner_map)

    placed = (
        P(("groups", "tile", "sub"), "rep"),
        P(("groups", "tile", "sub"), "rep"),
        P("rep", "tile"),
        P("rep", "tile"),
        P("groups"),
    )
    return jax.shard_map(
        shards,
        mesh=mesh,
        in_specs=placed,
        out_specs=P("groups", "sub", ("tile", "rep")),
        check_vma=False,
    )
```

```python
import functools

import jax
import jax.numpy as jnp
from jax import lax
from jax.experimental import pallas as pl
from jax.experimental.pallas import tpu as pltpu
from jax.sharding import PartitionSpec as P

TILE = 128
CHUNKS = 4
MESH = pl.DeviceIdType.MESH


def expand_mask(mask):
    big = jnp.repeat(jnp.repeat(mask, TILE, axis=0), TILE, axis=1)
    return big.astype(jnp.bfloat16)


def from_root(block, axis, source):
    block = jnp.where(lax.axis_index(axis) == source, block, jnp.zeros_like(block))
    return lax.psum(block, axis)


def stepwise(amplitudes, amp_mask, integrals, int_mask, owner_map):
    masked_amp = amplitudes * expand_mask(amp_mask)
    masked_int = integrals * expand_mask(int_mask)
    results = []
    for step in range(owner_map.shape[0]):
        block_rows = from_root(masked_amp, "tile", owner_map[step])
        partial_value = jnp.dot(block_rows, masked_int, preferred_element_type=jnp.float32)
        summed = lax.psum_scatter(
            partial_value.astype(jnp.bfloat16), "rep", scatter_dimension=1, tiled=True
        )
        results.append(summed)
    return jnp.stack(results, axis=0)


def tile_scale(mask_ref, i, j, shape):
    return jnp.full(shape, mask_ref[i, j].astype(jnp.float32), jnp.float32).astype(jnp.bfloat16)


def gather_kernel(
    n, reps, owner_hbm, amp_mask_hbm, int_mask_hbm, amp_hbm, int_hbm, out_ref,
    owner, amp_mask, int_mask, blocks, ints, mine, sent, got, end_ints, help_mine, help_sent, help_got,
    load_sem, up_send, up_recv, down_send, down_recv, x_send, x_recv,
    int_send, int_recv, y_send, y_recv, sub_send, sub_recv, help_send, help_recv, back_send, back_recv,
):
    z = lax.axis_index("tile")
    x = lax.axis_index("rep")
    rows, depth = amp_hbm.shape
    part = rows // CHUNKS
    width = int_hbm.shape[1] // reps
    group, sub = lax.axis_index("groups"), lax.axis_index("sub")
    is_end = (z == 0) | (z == n - 1)
    is_helper = (z == 1) | (z == n - 2)
    helper = jnp.where(z == 0, 1, n - 2)
    end = jnp.where(z == 1, 0, n - 1)
    quarter = depth // 4
    slab = quarter // CHUNKS

    loads = [
        pltpu.make_async_copy(source, target, load_sem.at[2 + at])
        for at, (source, target) in enumerate(
            ((amp_mask_hbm, amp_mask), (int_mask_hbm, int_mask), (owner_hbm, owner)))
    ]
    for load in loads:
        load.start()
    load_amp = pltpu.make_async_copy(amp_hbm, blocks.at[z], load_sem.at[0])
    load_int = pltpu.make_async_copy(int_hbm, ints, load_sem.at[1])
    load_amp.start()
    load_int.start()

    barrier = pltpu.get_barrier_semaphore()

    @pl.when(z > 0)
    def _():
        pl.semaphore_signal(barrier, inc=1, device_id={"tile": z - 1}, device_id_type=MESH)

    @pl.when(z < n - 1)
    def _():
        pl.semaphore_signal(barrier, inc=1, device_id={"tile": z + 1}, device_id_type=MESH)

    for k in range(1, reps):
        pl.semaphore_signal(barrier, inc=1, device_id={"rep": lax.rem(x + k, reps)}, device_id_type=MESH)

    @pl.when(is_helper)
    def _():
        pl.semaphore_signal(barrier, inc=1, device_id={"groups": 1 - group}, device_id_type=MESH)
        pl.semaphore_signal(barrier, inc=1, device_id={"sub": 1 - sub}, device_id_type=MESH)

    pl.semaphore_wait(barrier, jnp.where(is_helper, 2, 0) + jnp.where(z > 0, 1, 0) + jnp.where(z < n - 1, 1, 0) + (reps - 1))

    def span(c):
        return pl.ds(pl.multiple_of(c * part, part), part)

    def up(b, c):
        piece = blocks.at[b, span(c)]
        return pltpu.make_async_remote_copy(
            src_ref=piece, dst_ref=piece, send_sem=up_send.at[b, c], recv_sem=up_recv.at[b, c],
            device_id={"tile": z + 1}, device_id_type=MESH)

    def down(b, c):
        piece = blocks.at[b, span(c)]
        return pltpu.make_async_remote_copy(
            src_ref=piece, dst_ref=piece, send_sem=down_send.at[b, c], recv_sem=down_recv.at[b, c],
            device_id={"tile": z - 1}, device_id_type=MESH)

    def across(k, b, c):
        return pltpu.make_async_remote_copy(
            src_ref=sent.at[k - 1, b, span(c)], dst_ref=got.at[k - 1, b, span(c)],
            send_sem=x_send.at[k - 1, b, c], recv_sem=x_recv.at[k - 1, b, c],
            device_id={"rep": lax.rem(x + k, reps)}, device_id_type=MESH)

    def slab_of(g, u, c):
        return pl.ds(pl.multiple_of((g * 2 + u) * quarter + c * slab, slab), slab)

    def to_helper(c):
        return pltpu.make_async_remote_copy(
            src_ref=ints.at[slab_of(group, sub, c)], dst_ref=end_ints.at[slab_of(group, sub, c)],
            send_sem=int_send.at[c], recv_sem=int_recv.at[c], device_id={"tile": helper}, device_id_type=MESH)

    def from_end(c):
        piece = end_ints.at[slab_of(group, sub, c)]
        return pltpu.make_async_remote_copy(
            src_ref=piece, dst_ref=piece,
            send_sem=int_send.at[c], recv_sem=int_recv.at[c], device_id={"tile": end}, device_id_type=MESH)

    def over_y(g, c):
        piece = end_ints.at[slab_of(g, sub, c)]
        return pltpu.make_async_remote_copy(
            src_ref=piece, dst_ref=piece, send_sem=y_send.at[c], recv_sem=y_recv.at[c],
            device_id={"groups": 1 - group}, device_id_type=MESH)

    def over_sub(k, u, c):
        piece = end_ints.at[slab_of(group if k == 0 else 1 - group, u, c)]
        return pltpu.make_async_remote_copy(
            src_ref=piece, dst_ref=piece, send_sem=sub_send.at[k, c], recv_sem=sub_recv.at[k, c],
            device_id={"sub": 1 - sub}, device_id_type=MESH)

    def help_across(c):
        return pltpu.make_async_remote_copy(
            src_ref=help_sent.at[span(c)], dst_ref=help_got.at[span(c)],
            send_sem=help_send.at[c], recv_sem=help_recv.at[c],
            device_id={"rep": 1 - x}, device_id_type=MESH)

    def back(b, to, c):
        return pltpu.make_async_remote_copy(
            src_ref=help_mine.at[span(c)], dst_ref=mine.at[b, span(c)],
            send_sem=back_send.at[c], recv_sem=back_recv.at[c],
            device_id={"tile": to}, device_id_type=MESH)

    def pass_on(c):
        over_y(1 - group, c).wait_recv()
        over_sub(1, sub, c).start()

    def help_compute(c):
        help_sent[span(c), :] = jnp.dot(
            blocks[z, span(c), :], end_ints[:, columns(1 - x)],
            preferred_element_type=jnp.float32).astype(jnp.bfloat16)
        help_across(c).start()
        help_mine[span(c), :] = jnp.dot(
            blocks[z, span(c), :], end_ints[:, columns(x)],
            preferred_element_type=jnp.float32).astype(jnp.bfloat16)

    def help_finish(c):
        help_across(c).wait_recv()
        total = help_mine[span(c), :].astype(jnp.float32) + help_got[span(c), :].astype(jnp.float32)
        help_mine[span(c), :] = total.astype(jnp.bfloat16)
        back(z, end, c).start()

    def mask_ints(i):
        for j in range(int_hbm.shape[1] // TILE):
            at = pl.ds(pl.multiple_of(i * TILE, TILE), TILE)
            here = slice(j * TILE, (j + 1) * TILE)
            ints[at, here] = ints[at, here] * tile_scale(int_mask, i, j, (TILE, TILE))

    def columns(r):
        return pl.ds(pl.multiple_of(r * width, width), width)

    def compute(b, c):
        for k in range(1, reps):
            sent[k - 1, b, span(c), :] = jnp.dot(
                blocks[b, span(c), :], ints[:, columns(lax.rem(x + k, reps))],
                preferred_element_type=jnp.float32).astype(jnp.bfloat16)
            across(k, b, c).start()
        mine[b, span(c), :] = jnp.dot(
            blocks[b, span(c), :], ints[:, columns(x)],
            preferred_element_type=jnp.float32).astype(jnp.bfloat16)

    def finish(b, c):
        total = mine[b, span(c), :].astype(jnp.float32)
        for k in range(1, reps):
            across(k, b, c).wait_recv()
            total = total + got[k - 1, b, span(c), :].astype(jnp.float32)
        mine[b, span(c), :] = total.astype(jnp.bfloat16)

    for load in loads:
        load.wait()

    tall = depth // TILE
    first = (group * 2 + sub) * (quarter // TILE)

    load_amp.wait()
    for c in range(CHUNKS):
        at = slice(c * part, (c + 1) * part)
        for j in range(depth // TILE):
            here = slice(j * TILE, (j + 1) * TILE)
            scale = tile_scale(amp_mask, c * part // TILE, j, (part, TILE))
            blocks[z, at, here] = blocks[z, at, here] * scale

        @pl.when(z < n - 2)
        def _():
            up(z, c).start()

        @pl.when(z > 1)
        def _():
            down(z, c).start()

    @pl.when(is_end)
    def _():
        load_int.wait()

        @pl.loop(0, quarter // TILE)
        def _(i):
            mask_ints(first + i)

        for c in range(CHUNKS):
            to_helper(c).start()

    @pl.when(jnp.logical_not(is_end))
    def _():
        load_int.wait()

        @pl.loop(0, quarter // TILE)
        def _(i):
            mask_ints(first + i)

    @pl.loop(quarter // TILE, tall)
    def _(i):
        mask_ints(lax.rem(first + i, tall))

    @pl.loop(0, CHUNKS)
    def _(c):
        compute(z, c)

    w = n - 1 - z

    def comes(far, d):
        return (far - d >= 0) & ((d > 1) | ((d == 1) & (far < n - 1)))

    def lower(d):
        return jnp.maximum(z - d, 0)

    def upper(d):
        return n - 1 - jnp.maximum(w - d, 0)

    def finish_all(d, c):
        @pl.when(d == 0)
        def _():
            finish(z, c)

        @pl.when(comes(z, d))
        def _():
            finish(lower(d), c)

        @pl.when(comes(w, d))
        def _():
            finish(upper(d), c)

    @pl.loop(1, n)
    def _(d):
        @pl.loop(0, CHUNKS)
        def _(c):
            @pl.when(comes(z, d))
            def _():
                up(lower(d), c).wait_recv()

                @pl.when(z < n - 1)
                def _():
                    up(lower(d), c).start()

            @pl.when(comes(w, d))
            def _():
                down(upper(d), c).wait_recv()

                @pl.when(z > 0)
                def _():
                    down(upper(d), c).start()

            @pl.when(is_helper & (d == 2))
            def _():
                from_end(c).wait_recv()
                over_y(group, c).start()
                over_sub(0, sub, c).start()

            @pl.when(is_helper & (d == 2) & (c > 0))
            def _():
                pass_on(c - 1)

            @pl.when(comes(z, d))
            def _():
                compute(lower(d), c)

            @pl.when(comes(w, d))
            def _():
                compute(upper(d), c)

            @pl.when(is_helper & (d == 3))
            def _():
                @pl.when(c == 0)
                def _():
                    for piece in range(CHUNKS):
                        over_sub(0, 1 - sub, piece).wait_recv()
                        over_sub(1, 1 - sub, piece).wait_recv()

                help_compute(c)

                @pl.when(c > 0)
                def _():
                    help_finish(c - 1)

            finish_all(d - 1, c)

        @pl.when(is_helper & (d == 2))
        def _():
            pass_on(CHUNKS - 1)

        @pl.when(is_helper & (d == 3))
        def _():
            help_finish(CHUNKS - 1)

    @pl.loop(0, CHUNKS)
    def _(c):
        finish_all(n - 1, c)

        @pl.when(is_end)
        def _():
            back(helper, helper, c).wait_recv()

    for step in range(out_ref.shape[0]):
        out_ref[step] = mine[owner[step]]

    @pl.loop(0, n)
    def _(b):
        @pl.loop(0, CHUNKS)
        def _(c):
            @pl.when(jnp.logical_not(is_end & (b == helper)))
            def _():
                for k in range(1, reps):
                    across(k, b, c).wait_send()

            @pl.when((b <= z) & (z < n - 1) & (b != n - 2))
            def _():
                up(b, c).wait_send()

            @pl.when((b >= z) & (z > 0) & (b != 1))
            def _():
                down(b, c).wait_send()

    @pl.loop(0, CHUNKS)
    def _(c):
        @pl.when(is_end)
        def _():
            to_helper(c).wait_send()

        @pl.when(is_helper)
        def _():
            over_y(group, c).wait_send()
            over_sub(0, sub, c).wait_send()
            over_sub(1, sub, c).wait_send()
            help_across(c).wait_send()
            back(z, end, c).wait_send()


def gathered(n, reps, amplitudes, amp_mask, integrals, int_mask, owner_map):
    rows, depth = amplitudes.shape
    wide = integrals.shape[1]
    width = wide // reps
    steps = owner_map.shape[0]
    dma = pltpu.SemaphoreType.DMA
    bf16 = jnp.bfloat16
    return pl.pallas_call(
        functools.partial(gather_kernel, n, reps),
        out_shape=jax.ShapeDtypeStruct((steps, rows, width), bf16),
        in_specs=[pl.BlockSpec(memory_space=pl.ANY)] * 5,
        out_specs=pl.BlockSpec(memory_space=pltpu.VMEM),
        scratch_shapes=[
            pltpu.SMEM(owner_map.shape, jnp.int32),
            pltpu.SMEM(amp_mask.shape, jnp.int32),
            pltpu.SMEM(int_mask.shape, jnp.int32),
            pltpu.VMEM((n, rows, depth), bf16),
            pltpu.VMEM((depth, wide), bf16),
            pltpu.VMEM((n, rows, width), bf16),
            pltpu.VMEM((reps - 1, n, rows, width), bf16),
            pltpu.VMEM((reps - 1, n, rows, width), bf16),
            pltpu.VMEM((depth, wide), bf16),
            pltpu.VMEM((rows, width), bf16),
            pltpu.VMEM((rows, width), bf16),
            pltpu.VMEM((rows, width), bf16),
            dma((5,)),
            dma((n, CHUNKS)), dma((n, CHUNKS)), dma((n, CHUNKS)), dma((n, CHUNKS)),
            dma((reps - 1, n, CHUNKS)), dma((reps - 1, n, CHUNKS)),
            dma((CHUNKS,)), dma((CHUNKS,)), dma((CHUNKS,)), dma((CHUNKS,)),
            dma((2, CHUNKS)), dma((2, CHUNKS)),
            dma((CHUNKS,)), dma((CHUNKS,)), dma((CHUNKS,)), dma((CHUNKS,)),
        ],
        compiler_params=pltpu.CompilerParams(
            collective_id=0, has_side_effects=True, vmem_limit_bytes=24 * 1024 * 1024),
        cost_estimate=pl.CostEstimate(
            flops=2 * n * rows * depth * wide, bytes_accessed=2 * (rows * depth + depth * wide + n * rows * width),
            transcendentals=0),
    )(*(pltpu.with_memory_space_constraint(each, pltpu.HBM)
        for each in (owner_map, amp_mask, int_mask, amplitudes, integrals)))


def solution(mesh):
    n, reps = mesh.shape["tile"], mesh.shape["rep"]
    pairs = mesh.shape["groups"] == mesh.shape["sub"] == reps == 2

    def shards(amplitudes, amp_mask, integrals, int_mask, owner_map):
        if n > owner_map.shape[0] or n != 4 or not pairs:
            return stepwise(amplitudes, amp_mask, integrals, int_mask, owner_map)
        return gathered(n, reps, amplitudes, amp_mask, integrals, int_mask, owner_map)

    placed = (
        P(("groups", "tile", "sub"), "rep"),
        P(("groups", "tile", "sub"), "rep"),
        P("rep", "tile"),
        P("rep", "tile"),
        P("groups"),
    )
    return jax.shard_map(
        shards,
        mesh=mesh,
        in_specs=placed,
        out_specs=P("groups", "sub", ("tile", "rep")),
        check_vma=False,
    )
```

```python
import functools

import jax
import jax.numpy as jnp
from jax import lax
from jax.experimental import pallas as pl
from jax.experimental.pallas import tpu as pltpu
from jax.sharding import PartitionSpec as P

TILE = 128
CHUNKS = 4
MESH = pl.DeviceIdType.MESH


def expand_mask(mask):
    big = jnp.repeat(jnp.repeat(mask, TILE, axis=0), TILE, axis=1)
    return big.astype(jnp.bfloat16)


def from_root(block, axis, source):
    block = jnp.where(lax.axis_index(axis) == source, block, jnp.zeros_like(block))
    return lax.psum(block, axis)


def stepwise(amplitudes, amp_mask, integrals, int_mask, owner_map):
    masked_amp = amplitudes * expand_mask(amp_mask)
    masked_int = integrals * expand_mask(int_mask)
    results = []
    for step in range(owner_map.shape[0]):
        block_rows = from_root(masked_amp, "tile", owner_map[step])
        partial_value = jnp.dot(block_rows, masked_int, preferred_element_type=jnp.float32)
        summed = lax.psum_scatter(
            partial_value.astype(jnp.bfloat16), "rep", scatter_dimension=1, tiled=True
        )
        results.append(summed)
    return jnp.stack(results, axis=0)


def tile_scale(mask_ref, i, j, shape):
    return jnp.full(shape, mask_ref[i, j].astype(jnp.float32), jnp.float32).astype(jnp.bfloat16)


def gather_kernel(
    n, reps, owner_hbm, amp_mask_hbm, int_mask_hbm, amp_hbm, int_hbm, out_ref,
    owner, amp_mask, int_mask, blocks, ints, mine, sent, got,
    load_sem, up_send, up_recv, down_send, down_recv, x_send, x_recv,
):
    z = lax.axis_index("tile")
    x = lax.axis_index("rep")
    rows, depth = amp_hbm.shape
    part = rows // CHUNKS
    width = int_hbm.shape[1] // reps

    loads = [
        pltpu.make_async_copy(source, target, load_sem.at[2 + at])
        for at, (source, target) in enumerate(
            ((amp_mask_hbm, amp_mask), (int_mask_hbm, int_mask), (owner_hbm, owner)))
    ]
    load_amp = pltpu.make_async_copy(amp_hbm, blocks.at[z], load_sem.at[0])
    load_int = pltpu.make_async_copy(int_hbm, ints, load_sem.at[1])

    load_amp.start()
    loads[0].start()
    barrier = pltpu.get_barrier_semaphore()

    @pl.when(z > 0)
    def _():
        pl.semaphore_signal(barrier, inc=1, device_id={"tile": z - 1}, device_id_type=MESH)

    @pl.when(z < n - 1)
    def _():
        pl.semaphore_signal(barrier, inc=1, device_id={"tile": z + 1}, device_id_type=MESH)

    for k in range(1, reps):
        pl.semaphore_signal(barrier, inc=1, device_id={"rep": lax.rem(x + k, reps)}, device_id_type=MESH)
    pl.semaphore_wait(barrier, jnp.where(z > 0, 1, 0) + jnp.where(z < n - 1, 1, 0) + (reps - 1))

    def span(c):
        return pl.ds(pl.multiple_of(c * part, part), part)

    def up(b, c):
        piece = blocks.at[b, span(c)]
        return pltpu.make_async_remote_copy(
            src_ref=piece, dst_ref=piece, send_sem=up_send.at[b, c], recv_sem=up_recv.at[b, c],
            device_id={"tile": z + 1}, device_id_type=MESH)

    def down(b, c):
        piece = blocks.at[b, span(c)]
        return pltpu.make_async_remote_copy(
            src_ref=piece, dst_ref=piece, send_sem=down_send.at[b, c], recv_sem=down_recv.at[b, c],
            device_id={"tile": z - 1}, device_id_type=MESH)

    def across(k, b, c):
        return pltpu.make_async_remote_copy(
            src_ref=sent.at[k - 1, b, span(c)], dst_ref=got.at[k - 1, b, span(c)],
            send_sem=x_send.at[k - 1, b, c], recv_sem=x_recv.at[k - 1, b, c],
            device_id={"rep": lax.rem(x + k, reps)}, device_id_type=MESH)

    def columns(r):
        return pl.ds(pl.multiple_of(r * width, width), width)

    def compute(b, c):
        for k in range(1, reps):
            sent[k - 1, b, span(c), :] = jnp.dot(
                blocks[b, span(c), :], ints[:, columns(lax.rem(x + k, reps))],
                preferred_element_type=jnp.float32).astype(jnp.bfloat16)
            across(k, b, c).start()
        mine[b, span(c), :] = jnp.dot(
            blocks[b, span(c), :], ints[:, columns(x)],
            preferred_element_type=jnp.float32).astype(jnp.bfloat16)

    def finish(b, c):
        total = mine[b, span(c), :].astype(jnp.float32)
        for k in range(1, reps):
            across(k, b, c).wait_recv()
            total = total + got[k - 1, b, span(c), :].astype(jnp.float32)
        mine[b, span(c), :] = total.astype(jnp.bfloat16)

    loads[0].wait()
    load_amp.wait()
    load_int.start()
    for load in loads[1:]:
        load.start()
    for c in range(CHUNKS):
        at = slice(c * part, (c + 1) * part)
        for j in range(depth // TILE):
            here = slice(j * TILE, (j + 1) * TILE)
            scale = tile_scale(amp_mask, c * part // TILE, j, (part, TILE))
            blocks[z, at, here] = blocks[z, at, here] * scale

        @pl.when(z < n - 1)
        def _():
            up(z, c).start()

        @pl.when(z > 0)
        def _():
            down(z, c).start()

    load_int.wait()
    for load in loads[1:]:
        load.wait()
    for j in range(int_hbm.shape[1] // TILE):
        here = slice(j * TILE, (j + 1) * TILE)

        @pl.loop(0, depth // TILE)
        def _(i):
            at = pl.ds(pl.multiple_of(i * TILE, TILE), TILE)
            ints[at, here] = ints[at, here] * tile_scale(int_mask, i, j, (TILE, TILE))

    @pl.loop(0, CHUNKS)
    def _(c):
        compute(z, c)

    @pl.loop(1, n)
    def _(d):
        lower, upper = z - d, z + d

        @pl.loop(0, CHUNKS)
        def _(c):
            @pl.when(lower >= 0)
            def _():
                up(lower, c).wait_recv()

                @pl.when(z < n - 1)
                def _():
                    up(lower, c).start()

            @pl.when(upper < n)
            def _():
                down(upper, c).wait_recv()

                @pl.when(z > 0)
                def _():
                    down(upper, c).start()

            @pl.when(lower >= 0)
            def _():
                compute(lower, c)

            @pl.when(upper < n)
            def _():
                compute(upper, c)

            @pl.when(lower + 1 >= 0)
            def _():
                finish(lower + 1, c)

            @pl.when((upper - 1 < n) & (d > 1))
            def _():
                finish(upper - 1, c)

    @pl.loop(0, CHUNKS)
    def _(c):
        @pl.when(z == n - 1)
        def _():
            finish(0, c)

        @pl.when(z == 0)
        def _():
            finish(n - 1, c)

    for step in range(out_ref.shape[0]):
        out_ref[step] = mine[owner[step]]

    @pl.loop(0, n)
    def _(b):
        @pl.loop(0, CHUNKS)
        def _(c):
            for k in range(1, reps):
                across(k, b, c).wait_send()

            @pl.when((b <= z) & (z < n - 1))
            def _():
                up(b, c).wait_send()

            @pl.when((b >= z) & (z > 0))
            def _():
                down(b, c).wait_send()


def gathered(n, reps, amplitudes, amp_mask, integrals, int_mask, owner_map):
    rows, depth = amplitudes.shape
    wide = integrals.shape[1]
    width = wide // reps
    steps = owner_map.shape[0]
    dma = pltpu.SemaphoreType.DMA
    bf16 = jnp.bfloat16
    return pl.pallas_call(
        functools.partial(gather_kernel, n, reps),
        out_shape=jax.ShapeDtypeStruct((steps, rows, width), bf16),
        in_specs=[pl.BlockSpec(memory_space=pl.ANY)] * 5,
        out_specs=pl.BlockSpec(memory_space=pltpu.VMEM),
        scratch_shapes=[
            pltpu.SMEM(owner_map.shape, jnp.int32),
            pltpu.SMEM(amp_mask.shape, jnp.int32),
            pltpu.SMEM(int_mask.shape, jnp.int32),
            pltpu.VMEM((n, rows, depth), bf16),
            pltpu.VMEM((depth, wide), bf16),
            pltpu.VMEM((n, rows, width), bf16),
            pltpu.VMEM((reps - 1, n, rows, width), bf16),
            pltpu.VMEM((reps - 1, n, rows, width), bf16),
            dma((5,)),
            dma((n, CHUNKS)), dma((n, CHUNKS)), dma((n, CHUNKS)), dma((n, CHUNKS)),
            dma((reps - 1, n, CHUNKS)), dma((reps - 1, n, CHUNKS)),
        ],
        compiler_params=pltpu.CompilerParams(
            collective_id=0, has_side_effects=True, vmem_limit_bytes=24 * 1024 * 1024),
        cost_estimate=pl.CostEstimate(
            flops=2 * n * rows * depth * wide, bytes_accessed=2 * (rows * depth + depth * wide + n * rows * width),
            transcendentals=0),
    )(*(pltpu.with_memory_space_constraint(each, pltpu.HBM)
        for each in (owner_map, amp_mask, int_mask, amplitudes, integrals)))


def solution(mesh):
    n, reps = mesh.shape["tile"], mesh.shape["rep"]

    def shards(amplitudes, amp_mask, integrals, int_mask, owner_map):
        if n > owner_map.shape[0]:
            return stepwise(amplitudes, amp_mask, integrals, int_mask, owner_map)
        return gathered(n, reps, amplitudes, amp_mask, integrals, int_mask, owner_map)

    placed = (
        P(("groups", "tile", "sub"), "rep"),
        P(("groups", "tile", "sub"), "rep"),
        P("rep", "tile"),
        P("rep", "tile"),
        P("groups"),
    )
    return jax.shard_map(
        shards,
        mesh=mesh,
        in_specs=placed,
        out_specs=P("groups", "sub", ("tile", "rep")),
        check_vma=False,
    )
```
